32 devices in a mesh: row: 4 (over z), col: 8 (over y, x, core).
Axes of the slice: x: 2, y: 2, z: 4, core: 2. Of those that a mesh axis runs over, the one named last changes fastest.
Arguments:
- tokens: bfloat16 [1024, 8192], P('row', 'col'), may hold values from -6 to 6
- cotangent: bfloat16 [1024, 8192], P('row', 'col'), may hold values from -6 to 6
- gate_weight: bfloat16 [8192, 14336], P('row', 'col'), may hold values from -0.1875 to 0.1875
- up_weight: bfloat16 [8192, 14336], P('row', 'col'), may hold values from -0.1875 to 0.1875
- down_weight: bfloat16 [14336, 8192], P('col', 'row'), may hold values from -0.125 to 0.125
- tile_mask: int32 [64, 112], replicated, may hold values from 0 to 1, as said below
Outputs:
- output: bfloat16 [1024, 8192], P('row', 'col')
- input_grad: bfloat16 [1024, 8192], P('row', 'col')
- gate_grad: bfloat16 [8192, 14336], P('row', 'col')
- up_grad: bfloat16 [8192, 14336], P('row', 'col')
- down_grad: bfloat16 [14336, 8192], P('col', 'row')
The draws below stay inside these ranges and needn't reach their ends.
Inputs may be any that keep to these rules, and one draw needn't show every extreme that they name: `tile_mask`: the mask is made of 4 x 8 blocks of 16 x 14 tiles (block (i, j) holds tile rows i * 16.. and tile columns j * 14..). Each block holds between 8 and 48 ones, some block exactly 48, and the whole mask exactly 896 ones.
All inputs are finite; a program needn't handle non-finite values.
Results may differ from the reference program's by a relative error of at most 0.013.
Values may be sent and summed in bfloat16 or wider, within the bound.
A program may use at most 256 MiB of HBM per device.

```python
import jax
import jax.numpy as jnp
from jax import lax

D = 8192
FF = 14336
BLK = 128
TOK_DEV = 256
TOKENS = 1024
DT = 64
FT = 112
DTD = 16
FTD = 14
TILES = 224
MEAN = 28
CAP = 48
LOW = 8
NNZ = 896
N_ROW = 4
N_COL = 8


def draw_tile_mask(key, part):
    grid_rows = DT // DTD
    grid_cols = FT // FTD
    devices = grid_rows * grid_cols
    slots = jnp.arange(devices, dtype=jnp.int32)
    base = jnp.where(slots % 4 == 0, CAP, jnp.where(slots % 4 == 1, LOW, MEAN)).astype(jnp.int32)
    counts = jax.random.permutation(jax.random.fold_in(key, 11), base)
    block_keys = jax.random.split(jax.random.fold_in(key, 23), devices)

    def one_block(block_key):
        return jax.random.permutation(block_key, TILES).astype(jnp.int32)
    ranks = jax.vmap(one_block)(block_keys)
    blocks = (ranks < counts[:, None]).astype(jnp.int32).reshape(grid_rows, grid_cols, DTD, FTD)
    return jnp.transpose(blocks, (0, 2, 1, 3)).reshape(DT, FT)


def steps_of(own_key, shape, cuts, smallest, top_value):
    def one(dim, shards_of):
        steps = jax.random.uniform(jax.random.fold_in(jax.random.fold_in(own_key, 6), dim), (shards_of,), jnp.float32, smallest / len(cuts), top_value / len(cuts))
        return jnp.repeat(jnp.exp(steps), shape[dim] // shards_of).reshape((-1,) + (1,) * (len(shape) - dim - 1))

    factor_of = one(*cuts[0])
    for cut in cuts[1:]:
        factor_of = factor_of * one(*cut)
    return factor_of


def centred(own_key, shape, scale, reach, cuts=(), kind=jnp.bfloat16):
    drawn = scale * jax.random.normal(own_key, shape, jnp.float32)
    if cuts:
        drawn = drawn * steps_of(own_key, shape, cuts, -0.22, 0.18)
    return jnp.clip(drawn, -reach, reach).astype(kind)


def setup_inputs(seed: int = 0) -> dict:
    keys = jax.random.split(jax.random.key(seed), 7)
    return {
        "tokens": centred(keys[0], (TOKENS, D), 1.0, 6.0, ((0, 4), (1, 8))),
        "cotangent": centred(keys[1], (TOKENS, D), 1.0, 6.0, ((0, 4), (1, 8))),
        "gate_weight": centred(keys[2], (D, FF), (D // 8) ** -0.5, 0.1875, ((0, 4), (1, 8))),
        "up_weight": centred(keys[3], (D, FF), (D // 8) ** -0.5, 0.1875, ((0, 4), (1, 8))),
        "down_weight": centred(keys[4], (FF, D), (FF // 8) ** -0.5, 0.125, ((0, 8), (1, 4))),
        "tile_mask": draw_tile_mask(jax.random.fold_in(keys[6], 71), 0),
    }


def reference(tokens, cotangent, gate_weight, up_weight, down_weight, tile_mask):
    flat_mask = tile_mask.reshape(-1).astype(jnp.int32)
    places = jnp.arange(DT * FT, dtype=jnp.int32)
    active = jnp.argsort((1 - flat_mask) * (DT * FT) + places)[:NNZ].astype(jnp.int32)
    tile_row = (active // FT).astype(jnp.int32)
    tile_col = (active % FT).astype(jnp.int32)
    group_seg = ((tile_col // FTD) * DT + tile_row).astype(jnp.int32)
    gate_tiles = gate_weight.reshape(DT, BLK, FT, BLK)[tile_row, :, tile_col, :].astype(jnp.float32)
    up_tiles = up_weight.reshape(DT, BLK, FT, BLK)[tile_row, :, tile_col, :].astype(jnp.float32)
    down_tiles = down_weight.reshape(FT, BLK, DT, BLK)[tile_col, :, tile_row, :].astype(jnp.float32)

    def by_cols(parts):
        summed = jax.ops.segment_sum(jnp.swapaxes(parts, 0, 1), tile_col, num_segments=FT)
        return jnp.transpose(summed, (1, 0, 2)).reshape(parts.shape[0], FF)

    def by_groups(parts):
        summed = jax.ops.segment_sum(jnp.swapaxes(parts, 0, 1), group_seg, num_segments=N_COL * DT)
        rounded = lax.optimization_barrier(summed.astype(jnp.bfloat16)).astype(jnp.float32)
        total = jnp.sum(rounded.reshape(N_COL, DT, parts.shape[0], BLK), axis=0)
        return jnp.transpose(total, (1, 0, 2)).reshape(parts.shape[0], D)

    def row_group(pair):
        tok_rows, cot_rows = pair
        count = tok_rows.shape[0]
        token_tiles = tok_rows.reshape(count, DT, BLK)[:, tile_row].astype(jnp.float32)
        gate = by_cols(jnp.einsum('tsk,skn->tsn', token_tiles, gate_tiles))
        upper = by_cols(jnp.einsum('tsk,skn->tsn', token_tiles, up_tiles))
        hidden = (jax.nn.silu(gate) * upper).astype(jnp.bfloat16)
        hidden_tiles = hidden.reshape(count, FT, BLK)[:, tile_col].astype(jnp.float32)
        output = by_groups(jnp.einsum('tsf,sfd->tsd', hidden_tiles, down_tiles)).astype(jnp.bfloat16)
        cot_tiles = cot_rows.reshape(count, DT, BLK)[:, tile_row].astype(jnp.float32)
        hidden_grad = by_cols(jnp.einsum('tsd,sfd->tsf', cot_tiles, down_tiles))
        sigmoid_gate = jax.nn.sigmoid(gate)
        gate_cot = (hidden_grad * upper * sigmoid_gate * (1.0 + gate * (1.0 - sigmoid_gate))).astype(jnp.bfloat16)
        up_cot = (hidden_grad * jax.nn.silu(gate)).astype(jnp.bfloat16)
        gate_back = gate_cot.reshape(count, FT, BLK)[:, tile_col].astype(jnp.float32)
        up_back = up_cot.reshape(count, FT, BLK)[:, tile_col].astype(jnp.float32)
        down_part = jnp.einsum('tsf,tsd->sfd', hidden_tiles, cot_tiles).astype(jnp.bfloat16)
        gate_part = jnp.einsum('tsk,tsn->skn', token_tiles, gate_back).astype(jnp.bfloat16)
        up_part = jnp.einsum('tsk,tsn->skn', token_tiles, up_back).astype(jnp.bfloat16)
        input_terms = jnp.einsum('tsn,skn->tsk', gate_back, gate_tiles) + jnp.einsum('tsn,skn->tsk', up_back, up_tiles)
        input_grad = by_groups(input_terms).astype(jnp.bfloat16)
        return output, input_grad, gate_part, up_part, down_part

    outputs, input_grads, gate_parts, up_parts, down_parts = lax.map(
        row_group, (tokens.reshape(N_ROW, TOK_DEV, D), cotangent.reshape(N_ROW, TOK_DEV, D)))
    gate_sum = jnp.sum(gate_parts.astype(jnp.float32), axis=0).astype(jnp.bfloat16)
    up_sum = jnp.sum(up_parts.astype(jnp.float32), axis=0).astype(jnp.bfloat16)
    down_sum = jnp.sum(down_parts.astype(jnp.float32), axis=0).astype(jnp.bfloat16)
    gate_grad = jnp.zeros((DT, FT, BLK, BLK), jnp.bfloat16).at[tile_row, tile_col].set(gate_sum)
    gate_grad = jnp.transpose(gate_grad, (0, 2, 1, 3)).reshape(D, FF)
    up_grad = jnp.zeros((DT, FT, BLK, BLK), jnp.bfloat16).at[tile_row, tile_col].set(up_sum)
    up_grad = jnp.transpose(up_grad, (0, 2, 1, 3)).reshape(D, FF)
    down_grad = jnp.zeros((FT, DT, BLK, BLK), jnp.bfloat16).at[tile_col, tile_row].set(down_sum)
    down_grad = jnp.transpose(down_grad, (0, 2, 1, 3)).reshape(FF, D)
    return (outputs.reshape(TOKENS, D), input_grads.reshape(TOKENS, D), gate_grad, up_grad, down_grad)
```

```python
import jax
import jax.numpy as jnp
from jax import lax
from jax.sharding import PartitionSpec as P

BLK = 128


def on_device(tokens, cotangent, gate_weight, up_weight, down_weight, tile_mask):
    row_count = lax.axis_size("row")
    col_count = lax.axis_size("col")
    row_index = lax.axis_index("row")
    col_index = lax.axis_index("col")
    tok_rows, tok_cols = tokens.shape
    block_rows, block_cols = gate_weight.shape
    row_tiles = block_rows // BLK
    col_tiles = block_cols // BLK
    piece = tok_rows // col_count
    all_rows = tok_rows * row_count
    f32, bf16 = jnp.float32, jnp.bfloat16

    block = lax.dynamic_slice(
        tile_mask, (row_index * row_tiles, col_index * col_tiles), (row_tiles, col_tiles)
    ).astype(bf16)
    spread_rows = (
        jnp.arange(block_rows)[:, None] // BLK == jnp.arange(row_tiles)[None, :]
    ).astype(bf16)
    spread_cols = (
        jnp.arange(col_tiles)[:, None] == jnp.arange(block_cols)[None, :] // BLK
    ).astype(bf16)
    wide = jnp.dot(block, spread_cols, preferred_element_type=f32).astype(bf16)
    full = jnp.dot(spread_rows, wide, preferred_element_type=f32).astype(bf16)
    wide_t = jnp.dot(spread_rows, block, preferred_element_type=f32).astype(bf16).T
    full_t = jnp.dot(spread_cols.T, wide_t, preferred_element_type=f32).astype(bf16)
    gate_w = jnp.where(full > 0, gate_weight, 0)
    up_w = jnp.where(full > 0, up_weight, 0)
    down_w = jnp.where(full_t > 0, down_weight, 0)

    def spread(x):
        x = lax.all_to_all(x, "col", split_axis=0, concat_axis=1, tiled=True)
        x = lax.all_to_all(x, "row", split_axis=1, concat_axis=0, tiled=True)
        return lax.all_gather(x, "col", axis=0, tiled=True)

    def collect(x):
        x = lax.psum_scatter(x, "col", scatter_dimension=0, tiled=True)
        x = lax.all_to_all(x, "row", split_axis=0, concat_axis=1, tiled=True)
        return lax.all_to_all(x, "col", split_axis=1, concat_axis=0, tiled=True)

    def nn(a, b):
        return lax.dot_general(a, b, (((1,), (0,)), ((), ())), preferred_element_type=f32)

    def nt(a, b):
        return lax.dot_general(a, b, (((1,), (1,)), ((), ())), preferred_element_type=f32)

    def tn(a, b):
        return lax.dot_general(a, b, (((0,), (0,)), ((), ())), preferred_element_type=f32)

    def row_sum(x):
        return lax.psum_scatter(x.astype(bf16), "row", scatter_dimension=0, tiled=True).astype(f32)

    def row_gather(x):
        return lax.all_gather(x, "row", axis=0, tiled=True)

    toks = spread(tokens)
    cots = spread(cotangent)
    gate = row_sum(nn(toks, gate_w))
    upper = row_sum(nn(toks, up_w))
    hidden_grad = row_sum(nt(cots, down_w))
    sig = jax.nn.sigmoid(gate)
    silu = gate * sig
    hidden = row_gather((silu * upper).astype(bf16))
    gate_cot = row_gather(
        (hidden_grad * upper * sig * (1.0 + gate * (1.0 - sig))).astype(bf16)
    )
    up_cot = row_gather((hidden_grad * silu).astype(bf16))
    output = collect(nn(hidden, down_w).astype(bf16))
    down_grad = jnp.where(full_t > 0, tn(hidden, cots), 0).astype(bf16)
    gate_grad = jnp.where(full > 0, tn(toks, gate_cot), 0).astype(bf16)
    input_grad = collect((nt(gate_cot, gate_w) + nt(up_cot, up_w)).astype(bf16))
    up_grad = jnp.where(full > 0, tn(toks, up_cot), 0).astype(bf16)
    return output, input_grad, gate_grad, up_grad, down_grad


def solution(mesh):
    return jax.shard_map(
        on_device,
        mesh=mesh,
        in_specs=(
            P("row", "col"),
            P("row", "col"),
            P("row", "col"),
            P("row", "col"),
            P("col", "row"),
            P(),
        ),
        out_specs=(
            P("row", "col"),
            P("row", "col"),
            P("row", "col"),
            P("row", "col"),
            P("col", "row"),
        ),
        check_vma=False,
    )
```

```python
import functools

import jax
import jax.numpy as jnp
from jax import lax
from jax.experimental import pallas as pl
from jax.experimental.pallas import tpu as pltpu
from jax.sharding import PartitionSpec as P

BLK = 128
CHUNK = 16
SKEW = 2
MESH = pl.DeviceIdType.MESH


def exchange_kernel(
    count, chunks, gate_ref, up_ref, hg_ref, out_ref, part, rs_send, rs_recv, bc_send, bc_recv
):
    me = lax.axis_index("row")
    last = count - 1
    ways = ((me, me - 1, me + 1), (last - me, me + 1, me - 1))
    own = (gate_ref, up_ref, hg_ref)
    f32, bf16 = jnp.float32, jnp.bfloat16

    def sum_copy(place, device):
        return pltpu.make_async_remote_copy(
            src_ref=part.at[place],
            dst_ref=part.at[place],
            send_sem=rs_send.at[place],
            recv_sem=rs_recv.at[place],
            device_id={"row": device},
            device_id_type=MESH,
        )

    def result_copy(place, device):
        return pltpu.make_async_remote_copy(
            src_ref=out_ref.at[:, place],
            dst_ref=out_ref.at[:, place],
            send_sem=bc_send.at[place],
            recv_sem=bc_recv.at[place],
            device_id={"row": device},
            device_id_type=MESH,
        )

    barrier = pltpu.get_barrier_semaphore()
    for ok, device in ((me > 0, me - 1), (me < last, me + 1)):

        @pl.when(ok)
        def _():
            pl.semaphore_signal(barrier, inc=1, device_id={"row": device}, device_id_type=MESH)

    ends = jnp.logical_or(me == 0, me == last)

    @pl.when(ends)
    def _():
        pl.semaphore_wait(barrier, 1)

    @pl.when(jnp.logical_not(ends))
    def _():
        pl.semaphore_wait(barrier, 2)

    def sums_of(way, step):
        pos, toward, away = ways[way]
        chunk = step - SKEW * (last - pos)
        place = way * chunks + jnp.clip(chunk, 0, chunks - 1)
        active = jnp.logical_and(chunk >= 0, chunk < chunks)

        @pl.when(jnp.logical_and(active, pos == last))
        def _():
            for k in range(3):
                part[place, k] = own[k][place]
            sum_copy(place, toward).start()

        @pl.when(jnp.logical_and(active, jnp.logical_and(pos > 0, pos < last)))
        def _():
            sum_copy(place, away).wait_recv()
            for k in range(3):
                part[place, k] = (part[place, k].astype(f32) + own[k][place].astype(f32)).astype(
                    bf16
                )
            sum_copy(place, toward).start()

        @pl.when(jnp.logical_and(active, pos == 0))
        def _():
            sum_copy(place, away).wait_recv()
            gate, upper, hidden_grad = (
                part[place, k].astype(f32) + own[k][place].astype(f32) for k in range(3)
            )
            sig = jax.nn.sigmoid(gate)
            silu = gate * sig
            out_ref[0, place] = (silu * upper).astype(bf16)
            out_ref[1, place] = (
                hidden_grad * upper * sig * (1.0 + gate * (1.0 - sig))
            ).astype(bf16)
            out_ref[2, place] = (hidden_grad * silu).astype(bf16)
            result_copy(place, away).start()

    def results_of(way, step):
        pos, toward, away = ways[way]
        chunk = step - SKEW * (last + pos)
        place = way * chunks + jnp.clip(chunk, 0, chunks - 1)
        active = jnp.logical_and(chunk >= 0, chunk < chunks)

        @pl.when(jnp.logical_and(active, pos > 0))
        def _():
            result_copy(place, toward).wait_recv()

        @pl.when(jnp.logical_and(active, jnp.logical_and(pos > 0, pos < last)))
        def _():
            result_copy(place, away).start()

    def one_step(step, carry):
        for way in range(2):
            results_of(way, step)
            sums_of(way, step)
        return carry

    lax.fori_loop(0, chunks + 2 * SKEW * last, one_step, 0)

    def sent(chunk, carry):
        for way in range(2):
            pos, toward, away = ways[way]
            place = way * chunks + chunk

            @pl.when(pos > 0)
            def _():
                sum_copy(place, toward).wait_send()

            @pl.when(pos < last)
            def _():
                result_copy(place, away).wait_send()

        return carry

    lax.fori_loop(0, chunks, sent, 0)


def exchange(gate, upper, hidden_grad):
    count = lax.axis_size("row")
    rows, cols = gate.shape
    places = rows // CHUNK
    chunks = places // 2
    shape = (places, CHUNK, cols)
    out = pl.pallas_call(
        functools.partial(exchange_kernel, count, chunks),
        out_shape=jax.ShapeDtypeStruct((3,) + shape, jnp.bfloat16),
        in_specs=[pl.BlockSpec(memory_space=pltpu.VMEM)] * 3,
        out_specs=pl.BlockSpec(memory_space=pltpu.VMEM),
        scratch_shapes=[pltpu.VMEM((places, 3, CHUNK, cols), jnp.bfloat16)]
        + [pltpu.SemaphoreType.DMA((places,))] * 4,
        compiler_params=pltpu.CompilerParams(
            collective_id=0, has_side_effects=True, vmem_limit_bytes=48 * 1024 * 1024
        ),
        cost_estimate=pl.CostEstimate(
            flops=40 * rows * cols, bytes_accessed=12 * rows * cols, transcendentals=rows * cols
        ),
    )(gate.reshape(shape), upper.reshape(shape), hidden_grad.reshape(shape))
    return tuple(out[k].reshape(rows, cols) for k in range(3))


def on_device(tokens, cotangent, gate_weight, up_weight, down_weight, tile_mask):
    row_count = lax.axis_size("row")
    col_count = lax.axis_size("col")
    row_index = lax.axis_index("row")
    col_index = lax.axis_index("col")
    tok_rows, tok_cols = tokens.shape
    block_rows, block_cols = gate_weight.shape
    row_tiles = block_rows // BLK
    col_tiles = block_cols // BLK
    piece = tok_rows // col_count
    all_rows = tok_rows * row_count
    f32, bf16 = jnp.float32, jnp.bfloat16

    block = lax.dynamic_slice(
        tile_mask, (row_index * row_tiles, col_index * col_tiles), (row_tiles, col_tiles)
    ).astype(bf16)
    spread_rows = (
        jnp.arange(block_rows)[:, None] // BLK == jnp.arange(row_tiles)[None, :]
    ).astype(bf16)
    spread_cols = (
        jnp.arange(col_tiles)[:, None] == jnp.arange(block_cols)[None, :] // BLK
    ).astype(bf16)
    wide = jnp.dot(block, spread_cols, preferred_element_type=f32).astype(bf16)
    full = jnp.dot(spread_rows, wide, preferred_element_type=f32).astype(bf16)
    wide_t = jnp.dot(spread_rows, block, preferred_element_type=f32).astype(bf16).T
    full_t = jnp.dot(spread_cols.T, wide_t, preferred_element_type=f32).astype(bf16)
    gate_w = jnp.where(full > 0, gate_weight, 0)
    up_w = jnp.where(full > 0, up_weight, 0)
    down_w = jnp.where(full_t > 0, down_weight, 0)

    both = jnp.stack([tokens, cotangent])
    both = lax.all_to_all(both, "col", split_axis=1, concat_axis=2, tiled=True)
    both = lax.all_to_all(both, "row", split_axis=2, concat_axis=1, tiled=True)
    toks = lax.all_gather(both[0], "col", axis=0, tiled=True)
    cots = lax.all_gather(both[1], "col", axis=0, tiled=True)

    def collect(x):
        x = lax.psum_scatter(x, "col", scatter_dimension=0, tiled=True)
        x = lax.all_to_all(x, "row", split_axis=0, concat_axis=1, tiled=True)
        return lax.all_to_all(x, "col", split_axis=1, concat_axis=0, tiled=True)

    def nn(a, b):
        return lax.dot_general(a, b, (((1,), (0,)), ((), ())), preferred_element_type=f32)

    def nt(a, b):
        return lax.dot_general(a, b, (((1,), (1,)), ((), ())), preferred_element_type=f32)

    def tn(a, b):
        return lax.dot_general(a, b, (((0,), (0,)), ((), ())), preferred_element_type=f32)

    hidden, gate_cot, up_cot = exchange(
        nn(toks, gate_w).astype(bf16), nn(toks, up_w).astype(bf16), nt(cots, down_w).astype(bf16)
    )
    output = collect(nn(hidden, down_w).astype(bf16))
    down_grad = jnp.where(full_t > 0, tn(hidden, cots), 0).astype(bf16)
    gate_grad = jnp.where(full > 0, tn(toks, gate_cot), 0).astype(bf16)
    input_grad = collect((nt(gate_cot, gate_w) + nt(up_cot, up_w)).astype(bf16))
    up_grad = jnp.where(full > 0, tn(toks, up_cot), 0).astype(bf16)
    return output, input_grad, gate_grad, up_grad, down_grad


def solution(mesh):
    return jax.shard_map(
        on_device,
        mesh=mesh,
        in_specs=(
            P("row", "col"),
            P("row", "col"),
            P("row", "col"),
            P("row", "col"),
            P("col", "row"),
            P(),
        ),
        out_specs=(
            P("row", "col"),
            P("row", "col"),
            P("row", "col"),
            P("row", "col"),
            P("col", "row"),
        ),
        check_vma=False,
    )
```

```python
import functools

import jax
import jax.numpy as jnp
from jax import lax
from jax.experimental import pallas as pl
from jax.experimental.pallas import tpu as pltpu
from jax.sharding import PartitionSpec as P

BLK = 128
CHUNK = 16
SKEW = 2
MESH = pl.DeviceIdType.MESH


def exchange_kernel(
    count, chunks, gate_ref, up_ref, hg_ref, out_ref, part, rs_send, rs_recv, bc_send, bc_recv
):
    me = lax.axis_index("row")
    last = count - 1
    ways = ((me, me - 1, me + 1), (last - me, me + 1, me - 1))
    own = (gate_ref, up_ref, hg_ref)
    f32, bf16 = jnp.float32, jnp.bfloat16

    def sum_copy(place, device):
        return pltpu.make_async_remote_copy(
            src_ref=part.at[place],
            dst_ref=part.at[place],
            send_sem=rs_send.at[place],
            recv_sem=rs_recv.at[place],
            device_id={"row": device},
            device_id_type=MESH,
        )

    def result_copy(place, device):
        return pltpu.make_async_remote_copy(
            src_ref=out_ref.at[:, place],
            dst_ref=out_ref.at[:, place],
            send_sem=bc_send.at[place],
            recv_sem=bc_recv.at[place],
            device_id={"row": device},
            device_id_type=MESH,
        )

    barrier = pltpu.get_barrier_semaphore()
    for ok, device in ((me > 0, me - 1), (me < last, me + 1)):

        @pl.when(ok)
        def _():
            pl.semaphore_signal(barrier, inc=1, device_id={"row": device}, device_id_type=MESH)

    ends = jnp.logical_or(me == 0, me == last)

    @pl.when(ends)
    def _():
        pl.semaphore_wait(barrier, 1)

    @pl.when(jnp.logical_not(ends))
    def _():
        pl.semaphore_wait(barrier, 2)

    def sums_of(way, step):
        pos, toward, away = ways[way]
        chunk = step - SKEW * (last - pos)
        place = way * chunks + jnp.clip(chunk, 0, chunks - 1)
        active = jnp.logical_and(chunk >= 0, chunk < chunks)

        @pl.when(jnp.logical_and(active, pos == last))
        def _():
            for k in range(3):
                part[place, k] = own[k][place]
            sum_copy(place, toward).start()

        @pl.when(jnp.logical_and(active, jnp.logical_and(pos > 0, pos < last)))
        def _():
            sum_copy(place, away).wait_recv()
            for k in range(3):
                part[place, k] = (part[place, k].astype(f32) + own[k][place].astype(f32)).astype(
                    bf16
                )
            sum_copy(place, toward).start()

        @pl.when(jnp.logical_and(active, pos == 0))
        def _():
            sum_copy(place, away).wait_recv()
            gate, upper, hidden_grad = (
                part[place, k].astype(f32) + own[k][place].astype(f32) for k in range(3)
            )
            sig = jax.nn.sigmoid(gate)
            silu = gate * sig
            out_ref[0, place] = (silu * upper).astype(bf16)
            out_ref[1, place] = (
                hidden_grad * upper * sig * (1.0 + gate * (1.0 - sig))
            ).astype(bf16)
            out_ref[2, place] = (hidden_grad * silu).astype(bf16)
            result_copy(place, away).start()

    def results_of(way, step):
        pos, toward, away = ways[way]
        chunk = step - SKEW * (last + pos)
        place = way * chunks + jnp.clip(chunk, 0, chunks - 1)
        active = jnp.logical_and(chunk >= 0, chunk < chunks)

        @pl.when(jnp.logical_and(active, pos > 0))
        def _():
            result_copy(place, toward).wait_recv()

        @pl.when(jnp.logical_and(active, jnp.logical_and(pos > 0, pos < last)))
        def _():
            result_copy(place, away).start()

    def one_step(step, carry):
        for way in range(2):
            results_of(way, step)
            sums_of(way, step)
        return carry

    lax.fori_loop(0, chunks + 2 * SKEW * last, one_step, 0)

    def sent(chunk, carry):
        for way in range(2):
            pos, toward, away = ways[way]
            place = way * chunks + chunk

            @pl.when(pos > 0)
            def _():
                sum_copy(place, toward).wait_send()

            @pl.when(pos < last)
            def _():
                result_copy(place, away).wait_send()

        return carry

    lax.fori_loop(0, chunks, sent, 0)


def exchange(gate, upper, hidden_grad):
    count = lax.axis_size("row")
    rows, cols = gate.shape
    places = rows // CHUNK
    chunks = places // 2
    shape = (places, CHUNK, cols)
    out = pl.pallas_call(
        functools.partial(exchange_kernel, count, chunks),
        out_shape=jax.ShapeDtypeStruct((3,) + shape, jnp.bfloat16),
        in_specs=[pl.BlockSpec(memory_space=pltpu.VMEM)] * 3,
        out_specs=pl.BlockSpec(memory_space=pltpu.VMEM),
        scratch_shapes=[pltpu.VMEM((places, 3, CHUNK, cols), jnp.bfloat16)]
        + [pltpu.SemaphoreType.DMA((places,))] * 4,
        compiler_params=pltpu.CompilerParams(
            collective_id=0, has_side_effects=True, vmem_limit_bytes=48 * 1024 * 1024
        ),
        cost_estimate=pl.CostEstimate(
            flops=40 * rows * cols, bytes_accessed=12 * rows * cols, transcendentals=rows * cols
        ),
    )(gate.reshape(shape), upper.reshape(shape), hidden_grad.reshape(shape))
    return tuple(out[k].reshape(rows, cols) for k in range(3))


def on_device(tokens, cotangent, gate_weight, up_weight, down_weight, tile_mask):
    row_count = lax.axis_size("row")
    col_count = lax.axis_size("col")
    row_index = lax.axis_index("row")
    col_index = lax.axis_index("col")
    tok_rows, tok_cols = tokens.shape
    block_rows, block_cols = gate_weight.shape
    row_tiles = block_rows // BLK
    col_tiles = block_cols // BLK
    piece = tok_rows // col_count
    all_rows = tok_rows * row_count
    f32, bf16 = jnp.float32, jnp.bfloat16

    block = lax.dynamic_slice(
        tile_mask, (row_index * row_tiles, col_index * col_tiles), (row_tiles, col_tiles)
    ).astype(bf16)
    spread_rows = (
        jnp.arange(block_rows)[:, None] // BLK == jnp.arange(row_tiles)[None, :]
    ).astype(bf16)
    spread_cols = (
        jnp.arange(col_tiles)[:, None] == jnp.arange(block_cols)[None, :] // BLK
    ).astype(bf16)
    wide = jnp.dot(block, spread_cols, preferred_element_type=f32).astype(bf16)
    full = jnp.dot(spread_rows, wide, preferred_element_type=f32).astype(bf16)
    wide_t = jnp.dot(spread_rows, block, preferred_element_type=f32).astype(bf16).T
    full_t = jnp.dot(spread_cols.T, wide_t, preferred_element_type=f32).astype(bf16)
    gate_w = jnp.where(full > 0, gate_weight, 0)
    up_w = jnp.where(full > 0, up_weight, 0)
    down_w = jnp.where(full_t > 0, down_weight, 0)

    def spread(x):
        x = lax.all_to_all(x, "col", split_axis=0, concat_axis=1, tiled=True)
        x = lax.all_to_all(x, "row", split_axis=1, concat_axis=0, tiled=True)
        return lax.all_gather(x, "col", axis=0, tiled=True)

    def col_sum(x):
        return lax.psum_scatter(x, "col", scatter_dimension=0, tiled=True)

    def home(x):
        x = lax.all_to_all(x, "row", split_axis=0, concat_axis=1, tiled=True)
        return lax.all_to_all(x, "col", split_axis=1, concat_axis=0, tiled=True)

    def nn(a, b):
        return lax.dot_general(a, b, (((1,), (0,)), ((), ())), preferred_element_type=f32)

    def nt(a, b):
        return lax.dot_general(a, b, (((1,), (1,)), ((), ())), preferred_element_type=f32)

    def tn(a, b):
        return lax.dot_general(a, b, (((0,), (0,)), ((), ())), preferred_element_type=f32)

    toks = spread(tokens)
    cots = spread(cotangent)
    hidden, gate_cot, up_cot = exchange(
        nn(toks, gate_w).astype(bf16), nn(toks, up_w).astype(bf16), nt(cots, down_w).astype(bf16)
    )
    output = home(col_sum(nn(hidden, down_w).astype(bf16)))
    in_sum = col_sum((nt(gate_cot, gate_w) + nt(up_cot, up_w)).astype(bf16))
    down_grad = jnp.where(full_t > 0, tn(hidden, cots), 0).astype(bf16)
    up_grad = jnp.where(full > 0, tn(toks, up_cot), 0).astype(bf16)
    gate_grad = jnp.where(full > 0, tn(toks, gate_cot), 0).astype(bf16)
    in_sum, down_grad, up_grad = lax.optimization_barrier((in_sum, down_grad, up_grad))
    input_grad = home(in_sum)
    return output, input_grad, gate_grad, up_grad, down_grad


def solution(mesh):
    return jax.shard_map(
        on_device,
        mesh=mesh,
        in_specs=(
            P("row", "col"),
            P("row", "col"),
            P("row", "col"),
            P("row", "col"),
            P("col", "row"),
            P(),
        ),
        out_specs=(
            P("row", "col"),
            P("row", "col"),
            P("row", "col"),
            P("row", "col"),
            P("col", "row"),
        ),
        check_vma=False,
    )
```

```python
import functools

import jax
import jax.numpy as jnp
from jax import lax
from jax.experimental import pallas as pl
from jax.experimental.pallas import tpu as pltpu
from jax.sharding import PartitionSpec as P

BLK = 128
CHUNK = 16
SKEW = 2
MESH = pl.DeviceIdType.MESH


def exchange_kernel(
    count, chunks, gate_ref, up_ref, hg_ref, out_ref, part, rs_send, rs_recv, bc_send, bc_recv
):
    me = lax.axis_index("row")
    last = count - 1
    ways = ((me, me - 1, me + 1), (last - me, me + 1, me - 1))
    own = (gate_ref, up_ref, hg_ref)
    f32, bf16 = jnp.float32, jnp.bfloat16

    def sum_copy(place, device):
        return pltpu.make_async_remote_copy(
            src_ref=part.at[place],
            dst_ref=part.at[place],
            send_sem=rs_send.at[place],
            recv_sem=rs_recv.at[place],
            device_id={"row": device},
            device_id_type=MESH,
        )

    def result_copy(place, device):
        return pltpu.make_async_remote_copy(
            src_ref=out_ref.at[:, place],
            dst_ref=out_ref.at[:, place],
            send_sem=bc_send.at[place],
            recv_sem=bc_recv.at[place],
            device_id={"row": device},
            device_id_type=MESH,
        )

    barrier = pltpu.get_barrier_semaphore()
    for ok, device in ((me > 0, me - 1), (me < last, me + 1)):

        @pl.when(ok)
        def _():
            pl.semaphore_signal(barrier, inc=1, device_id={"row": device}, device_id_type=MESH)

    ends = jnp.logical_or(me == 0, me == last)

    @pl.when(ends)
    def _():
        pl.semaphore_wait(barrier, 1)

    @pl.when(jnp.logical_not(ends))
    def _():
        pl.semaphore_wait(barrier, 2)

    def sums_of(way, step):
        pos, toward, away = ways[way]
        chunk = step - SKEW * (last - pos)
        place = way * chunks + jnp.clip(chunk, 0, chunks - 1)
        active = jnp.logical_and(chunk >= 0, chunk < chunks)

        @pl.when(jnp.logical_and(active, pos == last))
        def _():
            for k in range(3):
                part[place, k] = own[k][place]
            sum_copy(place, toward).start()

        @pl.when(jnp.logical_and(active, jnp.logical_and(pos > 0, pos < last)))
        def _():
            sum_copy(place, away).wait_recv()
            for k in range(3):
                part[place, k] = (part[place, k].astype(f32) + own[k][place].astype(f32)).astype(
                    bf16
                )
            sum_copy(place, toward).start()

        @pl.when(jnp.logical_and(active, pos == 0))
        def _():
            sum_copy(place, away).wait_recv()
            gate, upper, hidden_grad = (
                part[place, k].astype(f32) + own[k][place].astype(f32) for k in range(3)
            )
            sig = jax.nn.sigmoid(gate)
            silu = gate * sig
            out_ref[0, place] = (silu * upper).astype(bf16)
            out_ref[1, place] = (
                hidden_grad * upper * sig * (1.0 + gate * (1.0 - sig))
            ).astype(bf16)
            out_ref[2, place] = (hidden_grad * silu).astype(bf16)
            result_copy(place, away).start()

    def results_of(way, step):
        pos, toward, away = ways[way]
        chunk = step - SKEW * (last + pos)
        place = way * chunks + jnp.clip(chunk, 0, chunks - 1)
        active = jnp.logical_and(chunk >= 0, chunk < chunks)

        @pl.when(jnp.logical_and(active, pos > 0))
        def _():
            result_copy(place, toward).wait_recv()

        @pl.when(jnp.logical_and(active, jnp.logical_and(pos > 0, pos < last)))
        def _():
            result_copy(place, away).start()

    def one_step(step, carry):
        for way in range(2):
            results_of(way, step)
            sums_of(way, step)
        return carry

    lax.fori_loop(0, chunks + 2 * SKEW * last, one_step, 0)

    def sent(chunk, carry):
        for way in range(2):
            pos, toward, away = ways[way]
            place = way * chunks + chunk

            @pl.when(pos > 0)
            def _():
                sum_copy(place, toward).wait_send()

            @pl.when(pos < last)
            def _():
                result_copy(place, away).wait_send()

        return carry

    lax.fori_loop(0, chunks, sent, 0)


def exchange(gate, upper, hidden_grad):
    count = lax.axis_size("row")
    rows, cols = gate.shape
    places = rows // CHUNK
    chunks = places // 2
    shape = (places, CHUNK, cols)
    out = pl.pallas_call(
        functools.partial(exchange_kernel, count, chunks),
        out_shape=jax.ShapeDtypeStruct((3,) + shape, jnp.bfloat16),
        in_specs=[pl.BlockSpec(memory_space=pltpu.VMEM)] * 3,
        out_specs=pl.BlockSpec(memory_space=pltpu.VMEM),
        scratch_shapes=[pltpu.VMEM((places, 3, CHUNK, cols), jnp.bfloat16)]
        + [pltpu.SemaphoreType.DMA((places,))] * 4,
        compiler_params=pltpu.CompilerParams(
            collective_id=0, has_side_effects=True, vmem_limit_bytes=48 * 1024 * 1024
        ),
        cost_estimate=pl.CostEstimate(
            flops=40 * rows * cols, bytes_accessed=12 * rows * cols, transcendentals=rows * cols
        ),
    )(gate.reshape(shape), upper.reshape(shape), hidden_grad.reshape(shape))
    return tuple(out[k].reshape(rows, cols) for k in range(3))


def on_device(tokens, cotangent, gate_weight, up_weight, down_weight, tile_mask):
    row_count = lax.axis_size("row")
    col_count = lax.axis_size("col")
    row_index = lax.axis_index("row")
    col_index = lax.axis_index("col")
    tok_rows, tok_cols = tokens.shape
    block_rows, block_cols = gate_weight.shape
    row_tiles = block_rows // BLK
    col_tiles = block_cols // BLK
    piece = tok_rows // col_count
    all_rows = tok_rows * row_count
    f32, bf16 = jnp.float32, jnp.bfloat16

    block = lax.dynamic_slice(
        tile_mask, (row_index * row_tiles, col_index * col_tiles), (row_tiles, col_tiles)
    ).astype(bf16)
    spread_rows = (
        jnp.arange(block_rows)[:, None] // BLK == jnp.arange(row_tiles)[None, :]
    ).astype(bf16)
    spread_cols = (
        jnp.arange(col_tiles)[:, None] == jnp.arange(block_cols)[None, :] // BLK
    ).astype(bf16)
    wide = jnp.dot(block, spread_cols, preferred_element_type=f32).astype(bf16)
    full = jnp.dot(spread_rows, wide, preferred_element_type=f32).astype(bf16)
    wide_t = jnp.dot(spread_rows, block, preferred_element_type=f32).astype(bf16).T
    full_t = jnp.dot(spread_cols.T, wide_t, preferred_element_type=f32).astype(bf16)
    gate_w = jnp.where(full > 0, gate_weight, 0)
    up_w = jnp.where(full > 0, up_weight, 0)
    down_w = jnp.where(full_t > 0, down_weight, 0)

    def spread(x):
        x = lax.all_to_all(x, "col", split_axis=0, concat_axis=1, tiled=True)
        x = lax.all_to_all(x, "row", split_axis=1, concat_axis=0, tiled=True)
        return lax.all_gather(x, "col", axis=0, tiled=True)

    def col_sum(x):
        return lax.psum_scatter(x, "col", scatter_dimension=0, tiled=True)

    def home(x):
        x = lax.all_to_all(x, "row", split_axis=0, concat_axis=1, tiled=True)
        return lax.all_to_all(x, "col", split_axis=1, concat_axis=0, tiled=True)

    def nn(a, b):
        return lax.dot_general(a, b, (((1,), (0,)), ((), ())), preferred_element_type=f32)

    def nt(a, b):
        return lax.dot_general(a, b, (((1,), (1,)), ((), ())), preferred_element_type=f32)

    def tn(a, b):
        return lax.dot_general(a, b, (((0,), (0,)), ((), ())), preferred_element_type=f32)

    toks = spread(tokens)
    cots = spread(cotangent)
    hidden, gate_cot, up_cot = exchange(
        nn(toks, gate_w).astype(bf16), nn(toks, up_w).astype(bf16), nt(cots, down_w).astype(bf16)
    )
    output = home(col_sum(nn(hidden, down_w).astype(bf16)))
    in_sum = col_sum((nt(gate_cot, gate_w) + nt(up_cot, up_w)).astype(bf16))
    down_grad = jnp.where(full_t > 0, tn(hidden, cots), 0).astype(bf16)
    up_grad = jnp.where(full > 0, tn(toks, up_cot), 0).astype(bf16)
    gate_grad = jnp.where(full > 0, tn(toks, gate_cot), 0).astype(bf16)
    in_sum, output, down_grad, up_grad = lax.optimization_barrier(
        (in_sum, output, down_grad, up_grad)
    )
    input_grad = home(in_sum)
    return output, input_grad, gate_grad, up_grad, down_grad


def solution(mesh):
    return jax.shard_map(
        on_device,
        mesh=mesh,
        in_specs=(
            P("row", "col"),
            P("row", "col"),
            P("row", "col"),
            P("row", "col"),
            P("col", "row"),
            P(),
        ),
        out_specs=(
            P("row", "col"),
            P("row", "col"),
            P("row", "col"),
            P("row", "col"),
            P("col", "row"),
        ),
        check_vma=False,
    )
```
